512 devices in a mesh: replica: 8 (over y), shard: 64 (over z, x, core).
Axes of the slice: x: 4, y: 8, z: 8, core: 2. Of those that a mesh axis runs over, the one named last changes fastest.
Arguments:
- hidden_states: bfloat16 [131072, 7168], P(('replica', 'shard')), may hold values from -6 to 6
- latent_grad: bfloat16 [131072, 512], P(('replica', 'shard')), may hold values from -0.078125 to 0.078125
- left_factor: float32 [128, 256, 256], P('shard', 'replica'), may hold values from -2 to 45, as said below
- right_factor: float32 [128, 256, 256], P('shard', 'replica'), may hold values from -2 to 45, as said below
- left_root: bfloat16 [128, 256, 256], P('shard'), may hold values from -1 to 4, as said below
- right_root: bfloat16 [128, 256, 256], P('shard'), may hold values from -1 to 4, as said below
- block_owner: int32 [56], replicated, may hold values from 0 to 63, as said below
- block_slot: int32 [56], replicated, may hold values from 0 to 1, as said below
Outputs:
- new_left: float32 [128, 256, 256], P('shard', 'replica')
- new_right: float32 [128, 256, 256], P('shard', 'replica')
- update: float32 [2, 256, 7168], P(None, 'shard')
The draws below stay inside these ranges and needn't reach their ends.
Inputs may be any that keep to these rules, and one draw needn't show every extreme that they name: `block_owner`: no owner holds more than 2 blocks, and some owner holds exactly 2. `block_slot`: no two blocks have both the same owner and the same slot. `left_factor`: Symmetric. `right_factor`: Symmetric. `left_root`: Symmetric. `right_root`: Symmetric.
All inputs are finite; a program needn't handle non-finite values.
Results may differ from the reference program's by a relative error of at most 0.005.
Values may be sent and summed in bfloat16 or wider, within the bound.
A program may use at most 64 MiB of HBM per device.

```python
import math
import jax
import jax.numpy as jnp
from jax import lax

D = 7168
LAT = 512
BS = 256
TOK_DEV = 256
TOKENS = 131072
CAP = 2
N_REPLICA = 8
N_SHARD = 64


def plan_arrays(key):
    total_blocks = LAT // BS * (D // BS)
    positions = jnp.arange(total_blocks, dtype=jnp.int32)
    leading = positions < CAP
    owner_rank = jnp.where(leading, 0, 1 + (positions - CAP) % (N_SHARD - 1))
    slot_index = jnp.where(leading, positions, (positions - CAP) // (N_SHARD - 1))
    owner_perm = jax.random.permutation(jax.random.fold_in(key, 71), N_SHARD).astype(jnp.int32)
    block_perm = jax.random.permutation(jax.random.fold_in(key, 72), total_blocks).astype(jnp.int32)
    owners = jnp.zeros((total_blocks,), jnp.int32).at[block_perm].set(owner_perm[owner_rank])
    slots = jnp.zeros((total_blocks,), jnp.int32).at[block_perm].set(slot_index.astype(jnp.int32))
    return (owners, slots)


def draw_block_owner(key, part):
    return plan_arrays(key)[0]


def draw_block_slot(key, part):
    return plan_arrays(key)[1]


def symmetric_blocks(key, diag_low, diag_high, reach):
    total_slots = N_SHARD * CAP
    noise = jax.random.uniform(jax.random.fold_in(key, 5), (total_slots, BS, BS), jnp.float32, -reach, reach)
    noise = 0.5 * (noise + jnp.swapaxes(noise, 1, 2))
    diagonal = jnp.exp(jax.random.uniform(jax.random.fold_in(key, 6), (total_slots, BS), jnp.float32, math.log(diag_low), math.log(diag_high)))
    return noise + diagonal[:, :, None] * jnp.eye(BS, dtype=jnp.float32)[None, :, :]


def draw_left_factor(key, part):
    return symmetric_blocks(jax.random.fold_in(key, 11), 2.0, 20.0, 1.7 / BS ** 0.5)


def draw_right_factor(key, part):
    return symmetric_blocks(jax.random.fold_in(key, 12), 2.0, 20.0, 1.7 / BS ** 0.5)


def draw_left_root(key, part):
    return symmetric_blocks(jax.random.fold_in(key, 13), 0.5, 2.0, 1.0 / BS ** 0.5).astype(jnp.bfloat16)


def draw_right_root(key, part):
    return symmetric_blocks(jax.random.fold_in(key, 14), 0.5, 2.0, 1.0 / BS ** 0.5).astype(jnp.bfloat16)


def strengthened(entries, key, source, target, shards_of, factor):
    def block_of(dim):
        return (jnp.arange(entries.shape[dim]) // (entries.shape[dim] // shards_of)).reshape((-1,) + (1,) * (entries.ndim - 1 - dim))

    one_side = jax.random.permutation(key, shards_of)[block_of(target)]
    far = (block_of(target) + shards_of // 2) % shards_of
    return jnp.where((block_of(source) == one_side) | (block_of(source) == far), factor * entries, entries)


def block_scale(own_key, dims, shards, smallest, high):
    factor_of, own = 1.0, jax.random.fold_in(own_key, 6)
    for position, blocks in shards:
        heights = jnp.exp(jax.random.uniform(jax.random.fold_in(own, position), (blocks,), jnp.float32, smallest / len(shards), high / len(shards)))
        factor_of = factor_of * jnp.repeat(heights, dims[position] // blocks).reshape([-1 if axis == position else 1 for axis in range(len(dims))])
    return factor_of


def gaussian(own_key, dims, scale, bound, cuts=(), kind=jnp.bfloat16):
    entries = jax.random.normal(own_key, dims, jnp.float32) * scale
    if len(cuts) > 0:
        entries = block_scale(own_key, dims, cuts, -0.22, 0.18) * entries
    return jnp.clip(entries, min=-bound, max=bound).astype(kind)


def gaussian_with(own_key, dims, spread, most, pieces, heavy, held_as=jnp.bfloat16):
    result = spread * jax.random.normal(own_key, dims, jnp.float32)
    if pieces:
        result = result * block_scale(own_key, dims, pieces, -0.22, 0.18)
    return jnp.clip(strengthened(result, jax.random.fold_in(own_key, 3), *heavy), -most, most).astype(held_as)


def setup_inputs(seed: int = 0) -> dict:
    splits = jax.random.split(jax.random.key(seed), 9)
    hidden_states = gaussian(splits[0], (TOKENS, D), 1.0, 6.0, ((0, 512),))
    latent_grad = gaussian_with(splits[1], (TOKENS, LAT), (0.5 / (TOK_DEV * N_REPLICA * N_SHARD) ** 0.5), 0.078125, ((0, 512),), (0, 1, 512, 6.0))
    left_factor = draw_left_factor(jax.random.fold_in(splits[8], 71), 0)
    right_factor = draw_right_factor(jax.random.fold_in(splits[8], 71), 0)
    left_root = draw_left_root(jax.random.fold_in(splits[8], 71), 0)
    right_root = draw_right_root(jax.random.fold_in(splits[8], 71), 0)
    block_owner = draw_block_owner(jax.random.fold_in(splits[8], 71), 0)
    block_slot = draw_block_slot(jax.random.fold_in(splits[8], 71), 0)
    return dict(hidden_states=hidden_states, latent_grad=latent_grad, left_factor=left_factor, right_factor=right_factor, left_root=left_root, right_root=right_root, block_owner=block_owner, block_slot=block_slot)


decay_rate = 0.95
epsilon = 1e-06

def reference(hidden_states, latent_grad, left_factor, right_factor, left_root, right_root, block_owner, block_slot):
    groups = N_REPLICA * N_SHARD
    inputs = hidden_states.reshape(groups, TOK_DEV, D)
    cotangents = latent_grad.reshape(groups, TOK_DEV, LAT)

    def accumulate(total, pair):
        span_in, span_out = pair
        partial_value = jnp.dot(span_out.T, span_in, preferred_element_type=jnp.float32).astype(jnp.bfloat16)
        partial_value = lax.optimization_barrier(partial_value)
        return (total + partial_value.astype(jnp.float32), None)
    gradient, _ = lax.scan(accumulate, jnp.zeros((LAT, D), jnp.float32), (inputs, cotangents))
    row_blocks = LAT // BS
    col_blocks = D // BS
    count = row_blocks * col_blocks
    blocks = gradient.reshape(row_blocks, BS, col_blocks, BS).transpose(0, 2, 1, 3).reshape(count, BS, BS)
    slot_index = (block_owner * CAP + block_slot).astype(jnp.int32)
    slot_grad = jnp.zeros((N_SHARD * CAP, BS, BS), jnp.float32).at[slot_index].set(blocks)
    high = lax.Precision.HIGHEST
    new_left = decay_rate * left_factor + (1.0 - decay_rate) * jnp.einsum('cik,cjk->cij', slot_grad, slot_grad, precision=high)
    new_right = decay_rate * right_factor + (1.0 - decay_rate) * jnp.einsum('cki,ckj->cij', slot_grad, slot_grad, precision=high)
    rounded = lax.optimization_barrier(slot_grad.astype(jnp.bfloat16)).astype(jnp.float32)
    half_product = jnp.einsum('cik,ckj->cij', left_root.astype(jnp.float32), rounded, precision=high).astype(jnp.bfloat16)
    half_product = lax.optimization_barrier(half_product).astype(jnp.float32)
    shaped = jnp.einsum('cik,ckj->cij', half_product, right_root.astype(jnp.float32), precision=high)
    grad_scale = jnp.sqrt(lax.optimization_barrier(jnp.mean(slot_grad * slot_grad, axis=(1, 2))))
    shaped_scale = jnp.sqrt(lax.optimization_barrier(jnp.mean(shaped * shaped, axis=(1, 2))) + epsilon)
    grafted = shaped * (grad_scale / shaped_scale)[:, None, None]
    chosen = grafted[slot_index]
    update = chosen.reshape(row_blocks, col_blocks, BS, BS).transpose(0, 2, 1, 3).reshape(row_blocks, BS, D)
    return (new_left, new_right, update)
```

```python
import functools

import jax
import jax.numpy as jnp
from jax import lax
from jax.experimental import pallas as pl
from jax.experimental.pallas import tpu as pltpu
from jax.sharding import PartitionSpec as P

D = 7168
LAT = 512
BS = 256
TOK = 256
NX, NY, NZ = 4, 8, 8
NT = 8
HALF = 128
DECAY = 0.95
EPS = 1e-06

PARTS = (
    (0, "m", 5, 9),
    (1, "m", 19, 9),
    (0, "x", 0, 5),
    (1, "x", 14, 5),
)
MESH = pl.DeviceIdType.MESH
F32 = jnp.float32
BF16 = jnp.bfloat16


def chain_shapes():
    shapes = {}
    for p, (_, first, _, nj) in enumerate(PARTS):
        for stage in range(2):
            over = first if stage == 0 else ("x" if first == "m" else "m")
            n = NX if over == "x" else 8
            rows = LAT // n if stage == 0 else 16
            for step in range(n // 2):
                for d in range(2):
                    shapes[(p, stage, d, step)] = (rows // 2 if step == 0 else rows, nj * HALF)
    return shapes


CHAIN = chain_shapes()
KEYS = tuple(CHAIN)
INDEX = {key: k for k, key in enumerate(KEYS)}


def one_hot(rows, cols, match):
    r = lax.broadcasted_iota(jnp.int32, (rows, cols), 0)
    c = lax.broadcasted_iota(jnp.int32, (rows, cols), 1)
    return jnp.where(match(r, c), 1.0, 0.0).astype(BF16)


def mm(a, b, ca=1, cb=0):
    return lax.dot_general(a, b, (((ca,), (cb,)), ((), ())), preferred_element_type=F32)


def kernel(hidden, latent, left_root, right_root, slots, ggl, ggr, upd, *scratch):
    n = len(KEYS)
    sends, recvs, scratch = scratch[:n], scratch[n : 2 * n], scratch[2 * n :]
    np_ = len(PARTS)
    hc, scratch = scratch[:np_], scratch[np_:]
    prod, scratch = scratch[:np_], scratch[np_:]
    mid, scratch = scratch[:np_], scratch[np_:]
    (lat, lt, s3, r3, s2z, z2, s2x, x2, yg, gf, s4z, z4, s4x, x4,
     hsem, csem_s, csem_r, s3sem, a2a) = scratch

    y = lax.axis_index("replica")
    s = lax.axis_index("shard")
    xc = s % 8
    c = s % 2
    x = (s // 2) % 4
    z = s // 8

    def dev(xx=None, yy=None, zz=None, xcc=None):
        q = xc if xcc is None else xcc
        if xx is not None:
            q = xx * 2 + c
        return (y if yy is None else yy, (z if zz is None else zz) * 8 + q)

    partner = dev(xcc=x * 2 + (1 - c))

    def own_copies(p):
        _, _, j0, nj = PARTS[p]
        return [
            pltpu.make_async_copy(
                hidden.at[:, pl.ds(pl.multiple_of((j0 + k) * BS + c * HALF, HALF), HALF)],
                hc[p].at[pl.ds(0, TOK), pl.ds(k * HALF, HALF)],
                hsem.at[0, p],
            )
            for k in range(nj)
        ]

    def far_copies(p):
        _, _, j0, nj = PARTS[p]
        return [
            pltpu.make_async_remote_copy(
                hidden.at[:, pl.ds(pl.multiple_of((j0 + k) * BS + (1 - c) * HALF, HALF), HALF)],
                hc[p].at[pl.ds(TOK, TOK), pl.ds(k * HALF, HALF)],
                hsem.at[1, p],
                hsem.at[2, p],
                device_id=partner,
                device_id_type=MESH,
            )
            for k in range(nj)
        ]

    def all_own(p):
        wide = PARTS[p][3] * HALF
        return pltpu.make_async_copy(
            hidden.at[:, pl.ds(0, wide)], hc[p].at[pl.ds(0, TOK), :], hsem.at[0, p]
        )

    def all_far(p):
        wide = PARTS[p][3] * HALF
        return pltpu.make_async_remote_copy(
            hidden.at[:, pl.ds(0, wide)], hc[p].at[pl.ds(TOK, TOK), :],
            hsem.at[1, p], hsem.at[2, p], device_id=partner, device_id_type=MESH,
        )

    own_lat = pltpu.make_async_copy(latent, lat.at[0], hsem.at[0, np_])
    far_lat = pltpu.make_async_remote_copy(
        latent, lat.at[1], hsem.at[1, np_], hsem.at[2, np_],
        device_id=partner, device_id_type=MESH,
    )
    own_lat.start()
    own = [own_copies(p) for p in range(np_)]
    far = [far_copies(p) for p in range(np_)]
    for p in range(np_):
        for k in own[p]:
            k.start()

    barrier = pltpu.get_barrier_semaphore()
    for d in range(1, 8):
        for to in (dev(yy=(y + d) % 8), dev(zz=(z + d) % 8), dev(xcc=(xc + d) % 8)):
            pl.semaphore_signal(barrier, inc=1, device_id=to, device_id_type=MESH)
    pl.semaphore_wait(barrier, 21)

    far_lat.start()
    for p in range(np_):
        for k in far[p]:
            k.start()

    perm_a = one_hot(LAT, LAT, lambda r, k: k == (r % 2) * BS + r // 2)
    perm_b = one_hot(
        LAT, LAT,
        lambda r, k: k == (r % 2) * BS + (r // 128) * 64 + ((r // 2) % 8) * 8 + (r // 16) % 8,
    )
    own_lat.wait()
    lt[0, :, 0:TOK] = mm(perm_a, lat[0], 1, 1).astype(BF16)
    lt[1, :, 0:TOK] = mm(perm_b, lat[0], 1, 1).astype(BF16)
    far_lat.wait_recv()
    lt[0, :, TOK : 2 * TOK] = mm(perm_a, lat[1], 1, 1).astype(BF16)
    lt[1, :, TOK : 2 * TOK] = mm(perm_b, lat[1], 1, 1).astype(BF16)

    def axis_of(p, stage):
        group, first, _, _ = PARTS[p]
        over = first if stage == 0 else ("x" if first == "m" else "m")
        if over == "x":
            return 4, x, lambda v: dev(xx=v)
        if group == 0:
            return 8, y, lambda v: dev(yy=v)
        return 8, z, lambda v: dev(zz=v)

    def copy_of(p, stage, d, step):
        num, me, at = axis_of(p, stage)
        k = INDEX[(p, stage, d, step)]
        to = (me + 1) % num if d == 0 else (me + num - 1) % num
        return pltpu.make_async_remote_copy(
            sends[k], recvs[k], csem_s.at[k], csem_r.at[k],
            device_id=at(to), device_id_type=MESH,
        )

    def own_rows(p, stage, chunk, piece):
        if stage == 0:
            if PARTS[p][1] == "x":
                start = chunk * 128 + piece * 16
            else:
                start = piece * 128 + chunk * 16
            return prod[p][pl.ds(pl.multiple_of(start, 16), 16), :]
        return mid[p][pl.ds(pl.multiple_of(chunk * 16 + piece * 8, 8), 8), :]

    def send_step(p, stage, step):
        num, me, _ = axis_of(p, stage)
        unit = 16 if stage == 0 else 8
        rows = (LAT // num if stage == 0 else 16) // unit
        for d in range(2):
            k = INDEX[(p, stage, d, step)]
            far_by = num // 2 - step
            chunk = (me + far_by) % num if d == 0 else (me + num - far_by) % num
            low, high = (0, rows) if step > 0 else ((0, rows // 2) if d == 0 else (rows // 2, rows))
            if step > 0:
                copy_of(p, stage, d, step - 1).wait_recv()
            prev = recvs[INDEX[(p, stage, d, step - 1)]] if step > 0 else None
            prev_low, prev_high = (low, high) if step > 1 else ((0, rows // 2) if d == 0 else (rows // 2, rows))

            def emit(a, b, add):
                @pl.loop(a, b)
                def _(i):
                    value = own_rows(p, stage, chunk, i)
                    if add:
                        value = value + prev[
                            pl.ds(pl.multiple_of((i - prev_low) * unit, unit), unit), :
                        ].astype(F32)
                    sends[k][pl.ds(pl.multiple_of((i - low) * unit, unit), unit), :] = value.astype(
                        sends[k].dtype
                    )

            if step == 0:
                emit(low, high, False)
            else:
                emit(prev_low, prev_high, True)
                if low < prev_low:
                    emit(low, prev_low, False)
                if prev_high < high:
                    emit(prev_high, high, False)
            copy_of(p, stage, d, step).start()

    def finish(p, stage):
        num, me, _ = axis_of(p, stage)
        unit = 16 if stage == 0 else 8
        rows = (LAT // num if stage == 0 else 16) // unit
        last = num // 2 - 1
        for d in range(2):
            copy_of(p, stage, d, last).wait_recv()
        up = recvs[INDEX[(p, stage, 0, last)]]
        down = recvs[INDEX[(p, stage, 1, last)]]
        if stage == 0:
            @pl.loop(0, rows)
            def _(i):
                at = pl.ds(pl.multiple_of(i * unit, unit), unit)
                mid[p][at, :] = (
                    own_rows(p, stage, me, i) + up[at, :].astype(F32) + down[at, :].astype(F32)
                )
        else:
            group, _, j0, nj = PARTS[p]
            for half in range(2):
                total = (
                    own_rows(p, stage, me, half)
                    + up[half * 8 : half * 8 + 8, :]
                    + down[half * 8 : half * 8 + 8, :]
                )
                for k in range(nj):
                    row = 2 * (j0 + k - 14 * group)
                    for t in range(4):
                        s3[group, half * 4 + t, row : row + 2, :] = total[
                            2 * t : 2 * t + 2, k * HALF : (k + 1) * HALF
                        ]

    for p in range(np_):
        all_own(p).wait()
        all_far(p).wait_recv()
        group, _, _, nj = PARTS[p]
        prod[p][...] = mm(lt[group], hc[p][...])
        send_step(p, 0, 0)

    ms = [p for p in range(np_) if PARTS[p][1] == "m"]
    xs = [p for p in range(np_) if PARTS[p][1] == "x"]
    s3[:, :, 28:32, :] = jnp.zeros((2, 8, 4, HALF), F32)
    for p in ms:
        send_step(p, 0, 1)
    for p in xs:
        send_step(p, 0, 1)
    for p in ms:
        send_step(p, 0, 2)
    for p in ms:
        send_step(p, 0, 3)
    for p in xs:
        finish(p, 0)
        send_step(p, 1, 0)
    for p in xs:
        send_step(p, 1, 1)
    for p in ms:
        finish(p, 0)
        send_step(p, 1, 0)
    for p in ms:
        send_step(p, 1, 1)
    for p in xs:
        send_step(p, 1, 2)
    for p in xs:
        send_step(p, 1, 3)
    for p in ms:
        finish(p, 1)
    for p in xs:
        finish(p, 1)

    def s3_copy(group, d):
        me = z if group == 0 else y
        to = (me + d) % 8
        return pltpu.make_async_remote_copy(
            s3.at[group, to], r3.at[group, d - 1],
            s3sem.at[0, group, d - 1], s3sem.at[1, group, d - 1],
            device_id=dev(zz=to) if group == 0 else dev(yy=to), device_id_type=MESH,
        )

    for group in range(2):
        for d in range(1, 8):
            s3_copy(group, d).start()
    pieces = []
    for group in range(2):
        total = s3[group, z if group == 0 else y]
        for d in range(1, 8):
            s3_copy(group, d).wait_recv()
            total = total + r3[group, d - 1]
        pieces.append(total)
    piece = jnp.concatenate(pieces, axis=0).astype(BF16)

    def exchange(k, src, dst, me, at, whole=False):
        return [
            pltpu.make_async_remote_copy(
                src if whole else src.at[(me + d) % 8],
                dst.at[me],
                a2a.at[k, 0, d - 1], a2a.at[k, 1, d - 1],
                device_id=at((me + d) % 8), device_id_type=MESH,
            )
            for d in range(1, 8)
        ]

    slot_row = slots[0:1, :]
    dispatch = jnp.where(
        lax.broadcasted_iota(jnp.int32, (128, 64), 0) == slot_row, 1.0, 0.0
    ).astype(BF16)
    s2z[...] = mm(dispatch, piece).astype(BF16).reshape(8, 16, HALF)
    ex = exchange(0, s2z, z2, z, lambda v: dev(zz=v))
    for k in ex:
        k.start()
    z2[z] = s2z[z]
    regroup = one_hot(
        128, 128, lambda o, i: i == (o % 8) * 16 + (o // 16) * 2 + (o // 8) % 2
    )
    for k in ex:
        k.wait_recv()
    s2x[...] = mm(regroup, z2[...].reshape(128, HALF)).astype(BF16).reshape(8, 16, HALF)
    ex2 = exchange(1, s2x, x2, xc, lambda v: dev(xcc=v))
    for k in ex2:
        k.start()
    x2[xc] = s2x[xc]
    for k in ex2:
        k.wait_recv()
    ex3 = exchange(2, x2, yg, y, lambda v: dev(yy=v), whole=True)
    for k in ex3:
        k.start()
    yg[y] = x2[...]
    for k in ex3:
        k.wait_recv()
    for yy in range(8):
        for q in range(8):
            both = yg[yy, q].astype(F32)
            row = (q // 2) * 64 + yy * 8
            for slot in range(2):
                gf[slot, row : row + 8, (q % 2) * HALF : (q % 2 + 1) * HALF] = both[
                    slot * 8 : slot * 8 + 8, :
                ]

    pick_rows = one_hot(64, BS, lambda r, k: k == r * 4 + y % 4)
    lane_half = pl.ds(pl.multiple_of((y // 4) * HALF, HALF), HALF)
    for slot in range(2):
        g = gf[slot]
        half = mm(left_root[slot], g.astype(BF16)).astype(BF16)
        shaped = mm(half, right_root[slot])
        grad_scale = jnp.sqrt(jnp.sum(g * g, keepdims=True) * (1.0 / (BS * BS)))
        shaped_scale = jnp.sqrt(jnp.sum(shaped * shaped, keepdims=True) * (1.0 / (BS * BS)) + EPS)
        chosen = mm(mm(pick_rows, half).astype(BF16), right_root[slot, :, lane_half])
        back = chosen * (grad_scale / shaped_scale)
        s4z[:, slot * 8 : slot * 8 + 8, :] = back.reshape(8, 8, HALF)
    ex4 = exchange(3, s4z, z4, z, lambda v: dev(zz=v))
    for k in ex4:
        k.start()
    z4[z] = s4z[z]

    rows_here = one_hot(32, BS, lambda r, k: k == r + y * 32)
    for slot in range(2):
        g = gf[slot].astype(BF16)
        ggl[slot] = mm(mm(rows_here, g).astype(BF16), g, 1, 1)
        ggr[slot] = mm(mm(rows_here, g, 1, 1).astype(BF16), g)

    for k in ex4:
        k.wait_recv()
    everything = z4[...].reshape(8, 2, 8, HALF)
    for q in range(8):
        s4x[q] = everything[:, :, q, :].reshape(16, HALF)
    ex5 = exchange(4, s4x, x4, xc, lambda v: dev(xcc=v))
    for k in ex5:
        k.start()
    x4[xc] = s4x[xc]
    owner = slot_row // 2
    back_slot = jnp.where(slot_row < 0, -1, (owner % 8) * 16 + (owner // 8) * 2 + slot_row % 2)
    picker = jnp.where(
        lax.broadcasted_iota(jnp.int32, (128, 64), 0) == back_slot, 1.0, 0.0
    )
    for k in ex5:
        k.wait_recv()
    upd[y] = lax.dot_general(
        picker, x4[...].reshape(128, HALF), (((0,), (0,)), ((), ())),
        precision=lax.Precision.HIGHEST, preferred_element_type=F32,
    )
    ex6 = exchange(5, upd.at[y], upd, y, lambda v: dev(yy=v), whole=True)
    for k in ex6:
        k.start()
    for k in ex6:
        k.wait_recv()

    far_lat.wait_send()
    for p in range(np_):
        all_far(p).wait_send()
    for key in KEYS:
        copy_of(*key).wait_send()
    for group in range(2):
        for d in range(1, 8):
            s3_copy(group, d).wait_send()
    for e in (ex, ex2, ex3, ex4, ex5, ex6):
        for k in e:
            k.wait_send()


def local(
    hidden_states,
    latent_grad,
    left_factor,
    right_factor,
    left_root,
    right_root,
    block_owner,
    block_slot,
):
    flat = (block_owner * 2 + block_slot).reshape(2, 2, 14).transpose(1, 2, 0).reshape(2, 28)
    slots = jnp.pad(flat, ((0, 0), (0, 4)), constant_values=-1).reshape(1, 64)
    slots = jnp.broadcast_to(slots, (8, 64))
    dtype_of = lambda key: BF16 if key[1] == 0 else F32
    bufs = [pltpu.VMEM(CHAIN[key], dtype_of(key)) for key in KEYS]
    scratch = bufs + bufs
    for width_of in (lambda w: ((2 * TOK, w), BF16), lambda w: ((LAT, w), F32)):
        scratch = scratch + [pltpu.VMEM(*width_of(part[3] * HALF)) for part in PARTS]
    scratch = scratch + [
        pltpu.VMEM((128 if part[1] == "x" else 64, part[3] * HALF), F32) for part in PARTS
    ]
    scratch = scratch + [
        pltpu.VMEM((2, TOK, LAT), BF16),
        pltpu.VMEM((2, LAT, 2 * TOK), BF16),
        pltpu.VMEM((2, 8, 32, HALF), F32),
        pltpu.VMEM((2, 7, 32, HALF), F32),
        pltpu.VMEM((8, 16, HALF), BF16),
        pltpu.VMEM((8, 16, HALF), BF16),
        pltpu.VMEM((8, 16, HALF), BF16),
        pltpu.VMEM((8, 16, HALF), BF16),
        pltpu.VMEM((8, 8, 16, HALF), BF16),
        pltpu.VMEM((2, BS, BS), F32),
        pltpu.VMEM((8, 16, HALF), F32),
        pltpu.VMEM((8, 16, HALF), F32),
        pltpu.VMEM((8, 16, HALF), F32),
        pltpu.VMEM((8, 16, HALF), F32),
        pltpu.SemaphoreType.DMA((3, len(PARTS) + 1)),
        pltpu.SemaphoreType.DMA((len(KEYS),)),
        pltpu.SemaphoreType.DMA((len(KEYS),)),
        pltpu.SemaphoreType.DMA((2, 2, 7)),
        pltpu.SemaphoreType.DMA((6, 2, 7)),
    ]
    vmem = pl.BlockSpec(memory_space=pltpu.VMEM)
    anywhere = pl.BlockSpec(memory_space=pl.ANY)
    ggl, ggr, upd = pl.pallas_call(
        kernel,
        out_shape=(
            jax.ShapeDtypeStruct((2, 32, BS), F32),
            jax.ShapeDtypeStruct((2, 32, BS), F32),
            jax.ShapeDtypeStruct((8, 64, HALF), F32),
        ),
        in_specs=[anywhere, anywhere, vmem, vmem, vmem],
        out_specs=(vmem, vmem, vmem),
        scratch_shapes=scratch,
        compiler_params=pltpu.CompilerParams(
            collective_id=0, has_side_effects=True, vmem_limit_bytes=56 * 1024 * 1024
        ),
    )(hidden_states, latent_grad, left_root, right_root, slots)
    new_left = DECAY * left_factor + (1.0 - DECAY) * ggl
    new_right = DECAY * right_factor + (1.0 - DECAY) * ggr
    update = (
        upd.reshape(2, 4, 2, 32, HALF)[:, :, :, :28]
        .reshape(2, 4, 2, 14, 2, HALF)
        .transpose(4, 1, 2, 3, 0, 5)
        .reshape(2, 4, D)
    )
    return (new_left, new_right, update)


def solution(mesh):
    placed = (
        P(("replica", "shard"), None),
        P(("replica", "shard"), None),
        P("shard", "replica", None),
        P("shard", "replica", None),
        P("shard", None, None),
        P("shard", None, None),
        P(),
        P(),
    )
    return jax.shard_map(
        local,
        mesh=mesh,
        in_specs=placed,
        out_specs=(
            P("shard", "replica", None),
            P("shard", "replica", None),
            P(None, "shard", None),
        ),
        check_vma=False,
    )
```

```python
import jax
import jax.numpy as jnp
from jax import lax
from jax.experimental import pallas as pl
from jax.experimental.pallas import tpu as pltpu
from jax.sharding import PartitionSpec as P

D = 7168
LAT = 512
BS = 256
TOK = 256
NX, NY, NZ = 4, 8, 8
NT = 8
HALF = 128
DECAY = 0.95
EPS = 1e-06

PAIRS = (("m", 6), ("x", 4), ("m", 4))
STARTS = tuple(sum(nj for _, nj in PAIRS[:k]) for k in range(len(PAIRS)))
PARTS = tuple(
    (group, first, start, nj)
    for (first, nj), start in zip(PAIRS, STARTS)
    for group in range(2)
)
SCHEDULE = (
    ("first", 0, 1),
    ("first", 1, 1),
    ("first", 2, 1),
    ("first", 0, 2),
    ("end", 1, 0),
    ("first", 2, 2),
    ("first", 0, 3),
    ("second", 1, 1),
    ("first", 2, 3),
    ("second", 1, 2),
    ("end", 0, 0),
    ("second", 1, 3),
    ("end", 2, 0),
    ("second", 0, 1),
    ("second", 2, 1),
    ("close", 1, 0),
    ("close", 0, 0),
    ("close", 2, 0),
)
FAR_FIRST = (4, 3, 5, 2, 6, 1, 7)
MESH = pl.DeviceIdType.MESH
F32 = jnp.float32
BF16 = jnp.bfloat16


def lanes_of(nj, d, step):
    cut = (nj + 1) // 2 * HALF
    if step > 0:
        return 0, nj * HALF
    return (0, cut) if d == 0 else (cut, nj * HALF)


def chain_shapes():
    shapes = {}
    for p, (_, first, _, nj) in enumerate(PARTS):
        for stage in range(2):
            over = first if stage == 0 else ("x" if first == "m" else "m")
            n = NX if over == "x" else 8
            for step in range(n // 2):
                for d in range(2):
                    if stage == 0:
                        rows = LAT // n // 2 if step == 0 else LAT // n
                        shapes[(p, stage, d, step)] = (rows, nj * HALF)
                    else:
                        low, high = lanes_of(nj, d, step)
                        shapes[(p, stage, d, step)] = (16, high - low)
    return shapes


CHAIN = chain_shapes()
KEYS = tuple(CHAIN)
INDEX = {key: k for k, key in enumerate(KEYS)}


def one_hot(rows, cols, match):
    r = lax.broadcasted_iota(jnp.int32, (rows, cols), 0)
    c = lax.broadcasted_iota(jnp.int32, (rows, cols), 1)
    return jnp.where(match(r, c), 1.0, 0.0).astype(BF16)


def mm(a, b, ca=1, cb=0):
    return lax.dot_general(a, b, (((ca,), (cb,)), ((), ())), preferred_element_type=F32)


def kernel(
    hidden, latent, left_factor, right_factor, left_root, right_root, owners, places,
    new_left, new_right, update, *scratch
):
    n = len(KEYS)
    sends, recvs, scratch = scratch[:n], scratch[n : 2 * n], scratch[2 * n :]
    np_ = len(PARTS)
    hc, scratch = scratch[:np_], scratch[np_:]
    prod, scratch = scratch[:np_], scratch[np_:]
    mid, scratch = scratch[:np_], scratch[np_:]
    (lat, lt, s3, r3, s2z, z2, s2x, x2, xs, yg, gf, s4z, s4b, z4, s5x, x4, upd,
     lf, rf, lroot, rroot,
     hsem, csem_s, csem_r, s3sem, a2a, psem) = scratch
    pend = []

    def send(copy):
        copy.start()
        pend.append(copy)

    y = lax.axis_index("replica")
    s = lax.axis_index("shard")
    xc = s % 8
    c = s % 2
    x = (s // 2) % 4
    z = s // 8

    ys = [(y + d) % 8 for d in range(8)]
    zs = [(z + d) % 8 for d in range(8)]
    cs = [(xc + d) % 8 for d in range(8)]
    xn = [(x + d) % 4 for d in range(4)]

    def dev(xx=None, yy=None, zz=None, xcc=None):
        q = xc if xcc is None else xcc
        if xx is not None:
            q = xx * 2 + c
        return (y if yy is None else yy, (z if zz is None else zz) * 8 + q)

    partner = dev(xcc=x * 2 + (1 - c))

    def columns(p, core):
        group, _, start, nj = PARTS[p]
        at = (group * 14 + start) * BS + core * (nj * HALF)
        return hidden.at[:, pl.ds(pl.multiple_of(at, HALF), nj * HALF)]

    def all_own(p):
        return pltpu.make_async_copy(columns(p, c), hc[p].at[pl.ds(0, TOK), :], hsem.at[0, p])

    def all_far(p):
        return pltpu.make_async_remote_copy(
            columns(p, 1 - c), hc[p].at[pl.ds(TOK, TOK), :],
            hsem.at[1, p], hsem.at[2, p], device_id=partner, device_id_type=MESH,
        )

    own_lat = pltpu.make_async_copy(latent, lat.at[0], hsem.at[0, np_])
    far_lat = pltpu.make_async_remote_copy(
        latent, lat.at[1], hsem.at[1, np_], hsem.at[2, np_],
        device_id=partner, device_id_type=MESH,
    )
    own_lat.start()
    params = [
        pltpu.make_async_copy(src, dst, psem.at[k])
        for k, (src, dst) in enumerate(
            ((left_root, lroot), (right_root, rroot), (left_factor, lf), (right_factor, rf))
        )
    ]
    for p in range(np_):
        all_own(p).start()
    for k in params:
        k.start()

    barrier = pltpu.get_barrier_semaphore()
    for d in FAR_FIRST:
        for to in (dev(yy=ys[d]), dev(zz=zs[d]), dev(xcc=cs[d])):
            pl.semaphore_signal(barrier, inc=1, device_id=to, device_id_type=MESH)
    pl.semaphore_wait(barrier, 21)

    send(far_lat)
    for p in range(np_):
        send(all_far(p))

    perm_a = one_hot(LAT, LAT, lambda r, k: k == (r % 2) * BS + r // 2)
    perm_b = one_hot(
        LAT, LAT,
        lambda r, k: k == (r % 2) * BS + (r // 128) * 64 + ((r // 2) % 8) * 8 + (r // 16) % 8,
    )
    own_lat.wait()
    lt[0, :, 0:TOK] = mm(perm_a, lat[0], 1, 1).astype(BF16)
    lt[1, :, 0:TOK] = mm(perm_b, lat[0], 1, 1).astype(BF16)
    far_lat.wait_recv()
    lt[0, :, TOK : 2 * TOK] = mm(perm_a, lat[1], 1, 1).astype(BF16)
    lt[1, :, TOK : 2 * TOK] = mm(perm_b, lat[1], 1, 1).astype(BF16)

    def axis_of(p, stage):
        group, first, _, _ = PARTS[p]
        over = first if stage == 0 else ("x" if first == "m" else "m")
        if over == "x":
            return 4, xn, lambda v: dev(xx=v)
        if group == 0:
            return 8, ys, lambda v: dev(yy=v)
        return 8, zs, lambda v: dev(zz=v)

    def copy_of(p, stage, d, step):
        num, me, at = axis_of(p, stage)
        k = INDEX[(p, stage, d, step)]
        to = me[1] if d == 0 else me[num - 1]
        return pltpu.make_async_remote_copy(
            sends[k], recvs[k], csem_s.at[k], csem_r.at[k],
            device_id=at(to), device_id_type=MESH,
        )

    def own_rows(p, chunk, piece):
        if PARTS[p][1] == "x":
            start = chunk * 128 + piece * 16
        else:
            start = piece * 128 + chunk * 16
        return prod[p][pl.ds(pl.multiple_of(start, 16), 16), :]

    def chunk_of(p, stage, d, step):
        num, me, _ = axis_of(p, stage)
        far_by = num // 2 - step
        return me[far_by] if d == 0 else me[num - far_by]

    def rows16(i):
        if not isinstance(i, int):
            i = pl.multiple_of(i * 16, 16)
            return pl.ds(i, 16)
        return pl.ds(i * 16, 16)

    def send_first(p, step):
        rows = LAT // axis_of(p, 0)[0] // 16
        for d in range(2):
            k = INDEX[(p, 0, d, step)]
            chunk = chunk_of(p, 0, d, step)
            half = (0, rows // 2) if d == 0 else (rows // 2, rows)
            rest = (rows // 2, rows) if d == 0 else (0, rows // 2)

            def emit(span, base, prev=None, prev_base=0):
                for i in range(*span):
                    value = own_rows(p, chunk, i)
                    if prev is not None:
                        value = value + prev[rows16(i - prev_base), :].astype(F32)
                    sends[k][rows16(i - base), :] = value.astype(BF16)

            if step == 0:
                emit(half, half[0])
            else:
                if step == 1:
                    emit(rest, 0)
                copy_of(p, 0, d, step - 1).wait_recv()
                prev = recvs[INDEX[(p, 0, d, step - 1)]]
                if step == 1:
                    emit(half, 0, prev, half[0])
                else:
                    emit((0, rows), 0, prev)
            send(copy_of(p, 0, d, step))

    def finish_first(p):
        num, me, _ = axis_of(p, 0)
        last = num // 2 - 1
        for d in range(2):
            copy_of(p, 0, d, last).wait_recv()
        up = recvs[INDEX[(p, 0, 0, last)]]
        down = recvs[INDEX[(p, 0, 1, last)]]

        for i in range(LAT // num // 16):
            at = rows16(i)
            mid[p][at, :] = own_rows(p, me[0], i) + up[at, :].astype(F32) + down[at, :].astype(F32)

    def send_second(p, step):
        nj = PARTS[p][3]
        for d in range(2):
            k = INDEX[(p, 1, d, step)]
            at = rows16(chunk_of(p, 1, d, step))
            kind = sends[k].dtype
            if step == 0:
                low, high = lanes_of(nj, d, 0)
                sends[k][...] = mid[p][at, low:high].astype(kind)
            else:
                copy_of(p, 1, d, step - 1).wait_recv()
                prev = recvs[INDEX[(p, 1, d, step - 1)]]
                if step == 1:
                    for e in range(2):
                        low, high = lanes_of(nj, e, 0)
                        value = mid[p][at, low:high]
                        if e == d:
                            value = value + prev[...].astype(F32)
                        sends[k][:, low:high] = value.astype(kind)
                else:
                    sends[k][...] = (mid[p][at, :] + prev[...].astype(F32)).astype(kind)
            send(copy_of(p, 1, d, step))

    def finish_second(p):
        num, me, _ = axis_of(p, 1)
        last = num // 2 - 1
        for d in range(2):
            copy_of(p, 1, d, last).wait_recv()
        up = recvs[INDEX[(p, 1, 0, last)]]
        down = recvs[INDEX[(p, 1, 1, last)]]
        group, _, j0, nj = PARTS[p]
        total = mid[p][rows16(me[0]), :] + up[...].astype(F32) + down[...].astype(F32)
        for k in range(nj):
            row = 2 * (j0 + k)
            for t in range(8):
                s3[group, t, row : row + 2, :] = total[
                    2 * t : 2 * t + 2, k * HALF : (k + 1) * HALF
                ]

    for p in range(np_):
        all_own(p).wait()
        all_far(p).wait_recv()
        group, _, _, nj = PARTS[p]
        prod[p][...] = mm(lt[group], hc[p][...])
        send_first(p, 0)

    s3[:, :, 28:32, :] = jnp.zeros((2, 8, 4, HALF), F32)
    for event, pair, step in SCHEDULE:
        for p in (2 * pair, 2 * pair + 1):
            if event == "first":
                send_first(p, step)
            elif event == "end":
                finish_first(p)
                send_second(p, 0)
            elif event == "second":
                send_second(p, step)
            else:
                finish_second(p)
    def s3_copy(group, d):
        to = zs[d] if group == 0 else ys[d]
        return pltpu.make_async_remote_copy(
            s3.at[group, to], r3.at[group, d - 1],
            s3sem.at[0, group, d - 1], s3sem.at[1, group, d - 1],
            device_id=dev(zz=to) if group == 0 else dev(yy=to), device_id_type=MESH,
        )

    for group in range(2):
        for d in FAR_FIRST:
            send(s3_copy(group, d))
    pieces = []
    for group in range(2):
        total = s3[group, z if group == 0 else y]
        for d in (1, 7, 2, 6, 3, 5, 4):
            s3_copy(group, d).wait_recv()
            total = total + r3[group, d - 1]
        pieces.append(total)
    piece = jnp.concatenate(pieces, axis=0).astype(BF16)

    def exchange(k, src, dst, me, at, whole=False):
        return [
            pltpu.make_async_remote_copy(
                src if whole else src.at[me[d]],
                dst.at[me[0]],
                a2a.at[k, 0, d - 1], a2a.at[k, 1, d - 1],
                device_id=at(me[d]), device_id_type=MESH,
            )
            for d in FAR_FIRST
        ]

    kk = lax.broadcasted_iota(jnp.int32, (8, 64), 1) % 32 // 2
    col = kk
    for (_, nj), start in zip(PAIRS, STARTS):
        inside = (kk >= start) & (kk < start + nj)
        col = jnp.where(inside, start + c * (nj // 2) + (kk - start) // 2, col)
    lane = lax.broadcasted_iota(jnp.int32, (8, 64), 1)
    block = jnp.where(kk < 14, (lane % 2) * 28 + (lane // 32) * 14 + col, -1)[0:1, :]
    to_rows = jnp.where(
        lax.broadcasted_iota(jnp.int32, (56, 64), 0) == block, 1.0, 0.0
    ).astype(BF16)
    flat = (owners[...] * 2 + places[...] + 1).astype(F32).astype(BF16)
    half_row = (mm(flat, to_rows).astype(jnp.int32) - 1) * 2 + kk[0:1, :] % 2
    dispatch = jnp.where(
        lax.broadcasted_iota(jnp.int32, (BS, 64), 0) == half_row, 1.0, 0.0
    ).astype(BF16)
    regroup = one_hot(
        BS, BS,
        lambda o, i: i == (o % 8) * 32 + (o // 32) * 4 + (o // 16) % 2 * 2 + (o // 8) % 2,
    )
    s2z[...] = mm(dispatch, piece).astype(BF16).reshape(8, 32, HALF)
    ex = exchange(0, s2z, z2, zs, lambda v: dev(zz=v))
    for k in ex:
        send(k)
    z2[z] = s2z[z]
    for k in ex:
        k.wait_recv()
    s2x[...] = mm(regroup, z2[...].reshape(BS, HALF)).astype(BF16).reshape(8, 32, HALF)
    ex2 = exchange(1, s2x, x2, cs, lambda v: dev(xcc=v))
    for k in ex2:
        send(k)
    x2[xc] = s2x[xc]
    for k in ex2:
        k.wait_recv()
    for q in range(4):
        xs[q] = (x2[2 * q].astype(F32) + x2[2 * q + 1].astype(F32)).astype(BF16)
    ex3 = exchange(2, xs, yg, ys, lambda v: dev(yy=v), whole=True)
    for k in ex3:
        send(k)
    yg[y] = xs[...]
    for k in ex3:
        k.wait_recv()
    for yy in range(8):
        for q in range(4):
            rows = yg[yy, q].astype(F32)
            for k in range(4):
                gf[
                    k // 2,
                    q * 64 + yy * 8 : q * 64 + yy * 8 + 8,
                    (k % 2) * HALF : (k % 2 + 1) * HALF,
                ] = rows[k * 8 : k * 8 + 8, :]

    for k in params:
        k.wait()
    pick_rows = one_hot(64, BS, lambda r, k: k == r * 4 + y % 4)
    lane_half = pl.ds(pl.multiple_of((y // 4) * HALF, HALF), HALF)
    for slot in range(2):
        g = gf[slot]
        product = mm(lroot[slot], g.astype(BF16))
        half = product.astype(BF16)
        low = (product - half.astype(F32)).astype(BF16)
        root = rroot[slot]
        shaped = mm(half, root) + mm(low, root)
        grad_scale = jnp.sqrt(jnp.sum(g * g, keepdims=True) * (1.0 / (BS * BS)))
        shaped_scale = jnp.sqrt(jnp.sum(shaped * shaped, keepdims=True) * (1.0 / (BS * BS)) + EPS)
        root = rroot[slot, :, lane_half]
        chosen = mm(mm(pick_rows, half).astype(BF16), root) + mm(mm(pick_rows, low).astype(BF16), root)
        back = chosen * (grad_scale / shaped_scale)
        s4z[:, slot * 8 : slot * 8 + 8, :] = back.reshape(8, 8, HALF)
    s4b[...] = s4z[...].astype(BF16)
    ex4 = exchange(3, s4b, z4, zs, lambda v: dev(zz=v))
    for k in ex4:
        send(k)
    z4[z] = s4b[z]

    rows_here = one_hot(32, BS, lambda r, k: k == r + y * 32)
    for slot in range(2):
        g = gf[slot].astype(BF16)
        new_left[slot] = DECAY * lf[slot] + (1.0 - DECAY) * mm(mm(rows_here, g).astype(BF16), g, 1, 1)
        new_right[slot] = DECAY * rf[slot] + (1.0 - DECAY) * mm(mm(rows_here, g, 1, 1).astype(BF16), g)
    regroup_back = one_hot(
        128, 128, lambda o, i: i == ((o // 2) % 8) * 16 + (o % 2) * 8 + o // 16
    )
    lane = lax.broadcasted_iota(jnp.int32, (8, 64), 1)
    block = jnp.where(lane < 56, lane, -1)[0:1, :]
    wide = jnp.where(
        lax.broadcasted_iota(jnp.int32, (56, 64), 0) == block, 1.0, 0.0
    ).astype(BF16)
    slot_row = mm(flat, wide).astype(jnp.int32) - 1
    owner = slot_row // 2
    back_slot = jnp.where(slot_row < 0, -1, (owner % 8) * 16 + (owner // 8) * 2 + slot_row % 2)
    picker = jnp.where(
        lax.broadcasted_iota(jnp.int32, (128, 64), 0) == back_slot, 1.0, 0.0
    ).astype(BF16)
    spread = one_hot(512, BS, lambda o, i: (o % 8 < 4) & (i == (o % 8) * 64 + o // 8))

    for k in ex4:
        k.wait_recv()
    s5x[...] = mm(regroup_back, z4[...].reshape(128, HALF)).astype(BF16).reshape(8, 16, HALF)
    ex5 = exchange(4, s5x, x4, cs, lambda v: dev(xcc=v))
    for k in ex5:
        send(k)
    x4[xc] = s5x[xc]
    for k in ex5:
        k.wait_recv()
    upd[y] = mm(picker, x4[...].reshape(128, HALF), 0, 0).astype(BF16)
    ex6 = exchange(5, upd.at[y], upd, ys, lambda v: dev(yy=v), whole=True)
    for k in ex6:
        send(k)
    for k in ex6:
        k.wait_recv()
    for h in range(2):
        tiles = mm(spread, upd[4 * h : 4 * h + 4].reshape(256, HALF))
        for j in range(28):
            for i in range(2):
                row = i * 28 + j
                update[i, :, j * BS + h * HALF : j * BS + (h + 1) * HALF] = tiles[
                    row * 8 : row * 8 + 4, :
                ]

    for k in pend:
        k.wait_send()


def move(a, b, c, to_a, to_b, to_c):
    to_a[...] = a[...]
    to_b[...] = b[...]
    to_c[...] = c[...]


def local(
    hidden_states,
    latent_grad,
    left_factor,
    right_factor,
    left_root,
    right_root,
    block_owner,
    block_slot,
):
    dtype_of = lambda key: BF16 if key[1] == 0 or PARTS[key[0]][1] == "m" else F32
    bufs = [pltpu.VMEM(CHAIN[key], dtype_of(key)) for key in KEYS]
    scratch = bufs + bufs
    for width_of in (lambda w: ((2 * TOK, w), BF16), lambda w: ((LAT, w), F32)):
        scratch = scratch + [pltpu.VMEM(*width_of(part[3] * HALF)) for part in PARTS]
    scratch = scratch + [
        pltpu.VMEM((128 if part[1] == "x" else 64, part[3] * HALF), F32) for part in PARTS
    ]
    scratch = scratch + [
        pltpu.VMEM((2, TOK, LAT), BF16),
        pltpu.VMEM((2, LAT, 2 * TOK), BF16),
        pltpu.VMEM((2, 8, 32, HALF), F32),
        pltpu.VMEM((2, 7, 32, HALF), F32),
        pltpu.VMEM((8, 32, HALF), BF16),
        pltpu.VMEM((8, 32, HALF), BF16),
        pltpu.VMEM((8, 32, HALF), BF16),
        pltpu.VMEM((8, 32, HALF), BF16),
        pltpu.VMEM((4, 32, HALF), BF16),
        pltpu.VMEM((8, 4, 32, HALF), BF16),
        pltpu.VMEM((2, BS, BS), F32),
        pltpu.VMEM((8, 16, HALF), F32),
        pltpu.VMEM((8, 16, HALF), BF16),
        pltpu.VMEM((8, 16, HALF), BF16),
        pltpu.VMEM((8, 16, HALF), BF16),
        pltpu.VMEM((8, 16, HALF), BF16),
        pltpu.VMEM((8, 64, HALF), BF16),
        pltpu.VMEM((2, 32, BS), F32),
        pltpu.VMEM((2, 32, BS), F32),
        pltpu.VMEM((2, BS, BS), BF16),
        pltpu.VMEM((2, BS, BS), BF16),
        pltpu.SemaphoreType.DMA((3, len(PARTS) + 1)),
        pltpu.SemaphoreType.DMA((len(KEYS),)),
        pltpu.SemaphoreType.DMA((len(KEYS),)),
        pltpu.SemaphoreType.DMA((2, 2, 7)),
        pltpu.SemaphoreType.DMA((6, 2, 7)),
        pltpu.SemaphoreType.DMA((4,)),
    ]
    vmem = pl.BlockSpec(memory_space=pltpu.VMEM)
    anywhere = pl.BlockSpec(memory_space=pl.ANY)
    results = pl.pallas_call(
        kernel,
        out_shape=(
            jax.ShapeDtypeStruct((2, 32, BS), F32),
            jax.ShapeDtypeStruct((2, 32, BS), F32),
            jax.ShapeDtypeStruct((2, 4, D), F32),
        ),
        in_specs=[anywhere] * 6 + [vmem, vmem],
        out_specs=(vmem, vmem, vmem),
        scratch_shapes=scratch,
        compiler_params=pltpu.CompilerParams(
            collective_id=0, has_side_effects=True, vmem_limit_bytes=56 * 1024 * 1024
        ),
    )(
        hidden_states,
        latent_grad,
        left_factor,
        right_factor,
        left_root,
        right_root,
        block_owner.reshape(1, 56),
        block_slot.reshape(1, 56),
    )
    return pl.pallas_call(
        move,
        out_shape=tuple(jax.ShapeDtypeStruct(r.shape, r.dtype) for r in results),
        in_specs=[vmem] * 3,
        out_specs=(vmem,) * 3,
    )(*results)


def solution(mesh):
    placed = (
        P(("replica", "shard"), None),
        P(("replica", "shard"), None),
        P("shard", "replica", None),
        P("shard", "replica", None),
        P("shard", None, None),
        P("shard", None, None),
        P(),
        P(),
    )
    return jax.shard_map(
        local,
        mesh=mesh,
        in_specs=placed,
        out_specs=(
            P("shard", "replica", None),
            P("shard", "replica", None),
            P(None, "shard", None),
        ),
        check_vma=False,
    )
```

```python
import jax
import jax.numpy as jnp
from jax import lax
from jax.experimental import pallas as pl
from jax.experimental.pallas import tpu as pltpu
from jax.sharding import PartitionSpec as P

D = 7168
LAT = 512
BS = 256
TOK = 256
NX, NY, NZ = 4, 8, 8
NT = 8
HALF = 128
DECAY = 0.95
EPS = 1e-06

PAIRS = (("m", 6), ("x", 2), ("m", 6))
STARTS = tuple(sum(nj for _, nj in PAIRS[:k]) for k in range(len(PAIRS)))
PARTS = tuple(
    (group, first, start, nj)
    for (first, nj), start in zip(PAIRS, STARTS)
    for group in range(2)
)
SCHEDULE = (
    ("first", 0, 1),
    ("first", 1, 1),
    ("first", 2, 1),
    ("first", 0, 2),
    ("end", 1, 0),
    ("first", 2, 2),
    ("first", 0, 3),
    ("first", 2, 3),
    ("end", 0, 0),
    ("end", 2, 0),
    ("second", 0, 1),
    ("second", 2, 1),
    ("close", 1, 0),
    ("close", 0, 0),
    ("close", 2, 0),
)
FAR_FIRST = (4, 3, 5, 2, 6, 1, 7)
MESH = pl.DeviceIdType.MESH
F32 = jnp.float32
BF16 = jnp.bfloat16


def lanes_of(nj, d, step):
    cut = (nj + 1) // 2 * HALF
    if step > 0:
        return 0, nj * HALF
    return (0, cut) if d == 0 else (cut, nj * HALF)


def chain_shapes():
    shapes = {}
    for p, (_, first, _, nj) in enumerate(PARTS):
        for stage in range(1 if first == "x" else 2):
            over = first if stage == 0 else ("x" if first == "m" else "m")
            n = NX if over == "x" else 8
            for step in range(n // 2):
                for d in range(2):
                    if stage == 0:
                        rows = LAT // n // 2 if step == 0 else LAT // n
                        shapes[(p, stage, d, step)] = (rows, nj * HALF)
                    else:
                        low, high = lanes_of(nj, d, step)
                        shapes[(p, stage, d, step)] = (16, high - low)
    return shapes


CHAIN = chain_shapes()
KEYS = tuple(CHAIN)
INDEX = {key: k for k, key in enumerate(KEYS)}


def one_hot(rows, cols, match):
    r = lax.broadcasted_iota(jnp.int32, (rows, cols), 0)
    c = lax.broadcasted_iota(jnp.int32, (rows, cols), 1)
    return jnp.where(match(r, c), 1.0, 0.0).astype(BF16)


def mm(a, b, ca=1, cb=0):
    return lax.dot_general(a, b, (((ca,), (cb,)), ((), ())), preferred_element_type=F32)


def kernel(
    hidden, latent, left_factor, right_factor, left_root, right_root, owners, places,
    new_left, new_right, update, *scratch
):
    n = len(KEYS)
    sends, recvs, scratch = scratch[:n], scratch[n : 2 * n], scratch[2 * n :]
    np_ = len(PARTS)
    hc, scratch = scratch[:np_], scratch[np_:]
    prod, scratch = scratch[:np_], scratch[np_:]
    mid, scratch = scratch[:np_], scratch[np_:]
    (lat, lt, s3, r3, s2z, z2, s2x, x2, xs, yg, gf, s4z, s4b, z4, s5x, x4, upd,
     lf, rf, lroot, rroot, d2, e2,
     hsem, csem_s, csem_r, s3sem, a2a, psem, s2sem) = scratch
    pend = []

    def send(copy):
        copy.start()
        pend.append(copy)

    def settle(count):
        for copy in pend[:count]:
            copy.wait_send()
        del pend[:count]

    y = lax.axis_index("replica")
    s = lax.axis_index("shard")
    xc = s % 8
    c = s % 2
    x = (s // 2) % 4
    z = s // 8

    ys = [(y + d) % 8 for d in range(8)]
    zs = [(z + d) % 8 for d in range(8)]
    cs = [(xc + d) % 8 for d in range(8)]
    xn = [(x + d) % 4 for d in range(4)]

    def dev(xx=None, yy=None, zz=None, xcc=None):
        q = xc if xcc is None else xcc
        if xx is not None:
            q = xx * 2 + c
        return (y if yy is None else yy, (z if zz is None else zz) * 8 + q)

    partner = dev(xcc=x * 2 + (1 - c))

    def columns(p, core):
        group, _, start, nj = PARTS[p]
        at = (group * 14 + start) * BS + core * (nj * HALF)
        return hidden.at[:, pl.ds(pl.multiple_of(at, HALF), nj * HALF)]

    def all_own(p):
        return pltpu.make_async_copy(columns(p, c), hc[p].at[pl.ds(0, TOK), :], hsem.at[0, p])

    def all_far(p):
        return pltpu.make_async_remote_copy(
            columns(p, 1 - c), hc[p].at[pl.ds(TOK, TOK), :],
            hsem.at[1, p], hsem.at[2, p], device_id=partner, device_id_type=MESH,
        )

    own_lat = pltpu.make_async_copy(latent, lat.at[0], hsem.at[0, np_])
    far_lat = pltpu.make_async_remote_copy(
        latent, lat.at[1], hsem.at[1, np_], hsem.at[2, np_],
        device_id=partner, device_id_type=MESH,
    )
    barrier = pltpu.get_barrier_semaphore()
    for d in FAR_FIRST:
        for to in (dev(yy=ys[d]), dev(zz=zs[d]), dev(xcc=cs[d])):
            pl.semaphore_signal(barrier, inc=1, device_id=to, device_id_type=MESH)
    own_lat.start()
    params = [
        pltpu.make_async_copy(src, dst, psem.at[k])
        for k, (src, dst) in enumerate(
            ((left_root, lroot), (right_root, rroot), (left_factor, lf), (right_factor, rf))
        )
    ]
    for p in range(np_):
        all_own(p).start()
    for k in params:
        k.start()

    perm_a = one_hot(LAT, LAT, lambda r, k: k == (r % 2) * BS + r // 2)
    perm_b = one_hot(
        LAT, LAT,
        lambda r, k: k == (r % 2) * BS + (r // 128) * 64 + ((r // 2) % 8) * 8 + (r // 16) % 8,
    )
    own_lat.wait()
    lt[0, :, 0:TOK] = mm(perm_a, lat[0], 1, 1).astype(BF16)
    lt[1, :, 0:TOK] = mm(perm_b, lat[0], 1, 1).astype(BF16)
    pl.semaphore_wait(barrier, 21)

    send(far_lat)
    for p in range(np_):
        send(all_far(p))

    far_lat.wait_recv()
    lt[0, :, TOK : 2 * TOK] = mm(perm_a, lat[1], 1, 1).astype(BF16)
    lt[1, :, TOK : 2 * TOK] = mm(perm_b, lat[1], 1, 1).astype(BF16)

    def axis_of(p, stage):
        group, first, _, _ = PARTS[p]
        over = first if stage == 0 else ("x" if first == "m" else "m")
        if over == "x":
            return 4, xn, lambda v: dev(xx=v)
        if group == 0:
            return 8, ys, lambda v: dev(yy=v)
        return 8, zs, lambda v: dev(zz=v)

    def copy_of(p, stage, d, step):
        num, me, at = axis_of(p, stage)
        k = INDEX[(p, stage, d, step)]
        to = me[1] if d == 0 else me[num - 1]
        return pltpu.make_async_remote_copy(
            sends[k], recvs[k], csem_s.at[k], csem_r.at[k],
            device_id=at(to), device_id_type=MESH,
        )

    def own_rows(p, chunk, piece):
        if PARTS[p][1] == "x":
            start = chunk * 128 + piece * 16
        else:
            start = piece * 128 + chunk * 16
        return prod[p][pl.ds(pl.multiple_of(start, 16), 16), :]

    def chunk_of(p, stage, d, step):
        num, me, _ = axis_of(p, stage)
        far_by = num // 2 - step
        return me[far_by] if d == 0 else me[num - far_by]

    def rows16(i):
        if not isinstance(i, int):
            i = pl.multiple_of(i * 16, 16)
            return pl.ds(i, 16)
        return pl.ds(i * 16, 16)

    def send_first(p, step):
        rows = LAT // axis_of(p, 0)[0] // 16
        for d in range(2):
            k = INDEX[(p, 0, d, step)]
            chunk = chunk_of(p, 0, d, step)
            half = (0, rows // 2) if d == 0 else (rows // 2, rows)
            rest = (rows // 2, rows) if d == 0 else (0, rows // 2)

            def emit(span, base, prev=None, prev_base=0):
                for i in range(*span):
                    value = own_rows(p, chunk, i)
                    if prev is not None:
                        value = value + prev[rows16(i - prev_base), :].astype(F32)
                    sends[k][rows16(i - base), :] = value.astype(BF16)

            if step == 0:
                emit(half, half[0])
            else:
                if step == 1:
                    emit(rest, 0)
                copy_of(p, 0, d, step - 1).wait_recv()
                prev = recvs[INDEX[(p, 0, d, step - 1)]]
                if step == 1:
                    emit(half, 0, prev, half[0])
                else:
                    emit((0, rows), 0, prev)
            send(copy_of(p, 0, d, step))

    def finish_first(p):
        num, me, _ = axis_of(p, 0)
        last = num // 2 - 1
        for d in range(2):
            copy_of(p, 0, d, last).wait_recv()
        up = recvs[INDEX[(p, 0, 0, last)]]
        down = recvs[INDEX[(p, 0, 1, last)]]

        for i in range(LAT // num // 16):
            at = rows16(i)
            mid[p][at, :] = own_rows(p, me[0], i) + up[at, :].astype(F32) + down[at, :].astype(F32)

    def direct(p, d):
        group = PARTS[p][0]
        _, me, at = axis_of(p, 1)
        return pltpu.make_async_remote_copy(
            d2.at[group, rows16(me[d])], e2.at[group, d - 1],
            s2sem.at[0, group, d - 1], s2sem.at[1, group, d - 1],
            device_id=at(me[d]), device_id_type=MESH,
        )

    def send_direct(p):
        d2[PARTS[p][0]] = mid[p][...].astype(BF16)
        for d in FAR_FIRST:
            send(direct(p, d))

    def send_second(p, step):
        nj = PARTS[p][3]
        for d in range(2):
            k = INDEX[(p, 1, d, step)]
            at = rows16(chunk_of(p, 1, d, step))
            kind = sends[k].dtype
            if step == 0:
                low, high = lanes_of(nj, d, 0)
                sends[k][...] = mid[p][at, low:high].astype(kind)
            else:
                copy_of(p, 1, d, step - 1).wait_recv()
                prev = recvs[INDEX[(p, 1, d, step - 1)]]
                if step == 1:
                    for e in range(2):
                        low, high = lanes_of(nj, e, 0)
                        value = mid[p][at, low:high]
                        if e == d:
                            value = value + prev[...].astype(F32)
                        sends[k][:, low:high] = value.astype(kind)
                else:
                    sends[k][...] = (mid[p][at, :] + prev[...].astype(F32)).astype(kind)
            send(copy_of(p, 1, d, step))

    def finish_second(p):
        num, me, _ = axis_of(p, 1)
        group, first, j0, nj = PARTS[p]
        total = mid[p][rows16(me[0]), :]
        if first == "x":
            for d in FAR_FIRST[::-1]:
                direct(p, d).wait_recv()
                total = total + e2[group, d - 1].astype(F32)
        else:
            last = num // 2 - 1
            for d in range(2):
                copy_of(p, 1, d, last).wait_recv()
                total = total + recvs[INDEX[(p, 1, d, last)]][...].astype(F32)
        for k in range(nj):
            row = 2 * (j0 + k)
            for t in range(8):
                s3[group, t, row : row + 2, :] = total[
                    2 * t : 2 * t + 2, k * HALF : (k + 1) * HALF
                ]

    for p in range(np_):
        all_own(p).wait()
        all_far(p).wait_recv()
        group, _, _, nj = PARTS[p]
        prod[p][...] = mm(lt[group], hc[p][...])
        send_first(p, 0)

    s3[:, :, 28:32, :] = jnp.zeros((2, 8, 4, HALF), F32)
    for event, pair, step in SCHEDULE:
        for p in (2 * pair, 2 * pair + 1):
            if event == "first":
                send_first(p, step)
            elif event == "end":
                finish_first(p)
                if PARTS[p][1] == "x":
                    send_direct(p)
                else:
                    send_second(p, 0)
            elif event == "second":
                send_second(p, step)
            else:
                finish_second(p)
    def s3_copy(group, d):
        to = zs[d] if group == 0 else ys[d]
        return pltpu.make_async_remote_copy(
            s3.at[group, to], r3.at[group, d - 1],
            s3sem.at[0, group, d - 1], s3sem.at[1, group, d - 1],
            device_id=dev(zz=to) if group == 0 else dev(yy=to), device_id_type=MESH,
        )

    for group in range(2):
        for d in FAR_FIRST:
            send(s3_copy(group, d))
    settle(len(pend) - 44)
    pieces = []
    for group in range(2):
        total = s3[group, z if group == 0 else y]
        for d in (1, 7, 2, 6, 3, 5, 4):
            s3_copy(group, d).wait_recv()
            total = total + r3[group, d - 1]
        pieces.append(total)
    piece = jnp.concatenate(pieces, axis=0).astype(BF16)

    def exchange(k, src, dst, me, at, whole=False):
        return [
            pltpu.make_async_remote_copy(
                src if whole else src.at[me[d]],
                dst.at[me[0]],
                a2a.at[k, 0, d - 1], a2a.at[k, 1, d - 1],
                device_id=at(me[d]), device_id_type=MESH,
            )
            for d in FAR_FIRST
        ]

    kk = lax.broadcasted_iota(jnp.int32, (8, 64), 1) % 32 // 2
    col = kk
    for (_, nj), start in zip(PAIRS, STARTS):
        inside = (kk >= start) & (kk < start + nj)
        col = jnp.where(inside, start + c * (nj // 2) + (kk - start) // 2, col)
    lane = lax.broadcasted_iota(jnp.int32, (8, 64), 1)
    block = jnp.where(kk < 14, (lane % 2) * 28 + (lane // 32) * 14 + col, -1)[0:1, :]
    to_rows = jnp.where(
        lax.broadcasted_iota(jnp.int32, (56, 64), 0) == block, 1.0, 0.0
    ).astype(BF16)
    flat = (owners[...] * 2 + places[...] + 1).astype(F32).astype(BF16)
    half_row = (mm(flat, to_rows).astype(jnp.int32) - 1) * 2 + kk[0:1, :] % 2
    dispatch = jnp.where(
        lax.broadcasted_iota(jnp.int32, (BS, 64), 0) == half_row, 1.0, 0.0
    ).astype(BF16)
    regroup = one_hot(
        BS, BS,
        lambda o, i: i == (o % 8) * 32 + (o // 32) * 4 + (o // 16) % 2 * 2 + (o // 8) % 2,
    )
    s2z[...] = mm(dispatch, piece).astype(BF16).reshape(8, 32, HALF)
    ex = exchange(0, s2z, z2, zs, lambda v: dev(zz=v))
    for k in ex:
        send(k)
    settle(len(pend) - 21)
    z2[z] = s2z[z]
    for k in ex:
        k.wait_recv()
    s2x[...] = mm(regroup, z2[...].reshape(BS, HALF)).astype(BF16).reshape(8, 32, HALF)
    ex2 = exchange(1, s2x, x2, cs, lambda v: dev(xcc=v))
    for k in ex2:
        send(k)
    settle(len(pend) - 7)
    x2[xc] = s2x[xc]
    for k in ex2:
        k.wait_recv()
    for q in range(4):
        xs[q] = (x2[2 * q].astype(F32) + x2[2 * q + 1].astype(F32)).astype(BF16)
    ex3 = exchange(2, xs, yg, ys, lambda v: dev(yy=v), whole=True)
    for k in ex3:
        send(k)
    settle(len(pend) - 7)
    yg[y] = xs[...]
    for k in ex3:
        k.wait_recv()
    for yy in range(8):
        for q in range(4):
            rows = yg[yy, q].astype(F32)
            for k in range(4):
                gf[
                    k // 2,
                    q * 64 + yy * 8 : q * 64 + yy * 8 + 8,
                    (k % 2) * HALF : (k % 2 + 1) * HALF,
                ] = rows[k * 8 : k * 8 + 8, :]

    for k in params:
        k.wait()
    pick_rows = one_hot(64, BS, lambda r, k: k == r * 4 + y % 4)
    lane_half = pl.ds(pl.multiple_of((y // 4) * HALF, HALF), HALF)
    for slot in range(2):
        g = gf[slot]
        product = mm(lroot[slot], g.astype(BF16))
        half = product.astype(BF16)
        low = (product - half.astype(F32)).astype(BF16)
        root = rroot[slot]
        shaped = mm(half, root) + mm(low, root)
        grad_scale = jnp.sqrt(jnp.sum(g * g, keepdims=True) * (1.0 / (BS * BS)))
        shaped_scale = jnp.sqrt(jnp.sum(shaped * shaped, keepdims=True) * (1.0 / (BS * BS)) + EPS)
        root = rroot[slot, :, lane_half]
        chosen = mm(mm(pick_rows, half).astype(BF16), root) + mm(mm(pick_rows, low).astype(BF16), root)
        back = chosen * (grad_scale / shaped_scale)
        s4z[:, slot * 8 : slot * 8 + 8, :] = back.reshape(8, 8, HALF)
    s4b[...] = s4z[...].astype(BF16)
    ex4 = exchange(3, s4b, z4, zs, lambda v: dev(zz=v))
    for k in ex4:
        send(k)
    settle(len(pend) - 7)
    z4[z] = s4b[z]

    rows_here = one_hot(32, BS, lambda r, k: k == r + y * 32)
    for slot in range(2):
        g = gf[slot].astype(BF16)
        new_left[slot] = DECAY * lf[slot] + (1.0 - DECAY) * mm(mm(rows_here, g).astype(BF16), g, 1, 1)
        new_right[slot] = DECAY * rf[slot] + (1.0 - DECAY) * mm(mm(rows_here, g, 1, 1).astype(BF16), g)
    regroup_back = one_hot(
        128, 128, lambda o, i: i == ((o // 2) % 8) * 16 + (o % 2) * 8 + o // 16
    )
    lane = lax.broadcasted_iota(jnp.int32, (8, 64), 1)
    block = jnp.where(lane < 56, lane, -1)[0:1, :]
    wide = jnp.where(
        lax.broadcasted_iota(jnp.int32, (56, 64), 0) == block, 1.0, 0.0
    ).astype(BF16)
    slot_row = mm(flat, wide).astype(jnp.int32) - 1
    owner = slot_row // 2
    back_slot = jnp.where(slot_row < 0, -1, (owner % 8) * 16 + (owner // 8) * 2 + slot_row % 2)
    picker = jnp.where(
        lax.broadcasted_iota(jnp.int32, (128, 64), 0) == back_slot, 1.0, 0.0
    ).astype(BF16)
    spread = one_hot(512, BS, lambda o, i: (o % 8 < 4) & (i == (o % 8) * 64 + o // 8))

    for k in ex4:
        k.wait_recv()
    s5x[...] = mm(regroup_back, z4[...].reshape(128, HALF)).astype(BF16).reshape(8, 16, HALF)
    ex5 = exchange(4, s5x, x4, cs, lambda v: dev(xcc=v))
    for k in ex5:
        send(k)
    settle(len(pend) - 7)
    x4[xc] = s5x[xc]
    for k in ex5:
        k.wait_recv()
    upd[y] = mm(picker, x4[...].reshape(128, HALF), 0, 0).astype(BF16)
    ex6 = exchange(5, upd.at[y], upd, ys, lambda v: dev(yy=v), whole=True)
    for k in ex6:
        send(k)
    settle(len(pend) - 7)
    for k in ex6:
        k.wait_recv()
    for h in range(2):
        tiles = mm(spread, upd[4 * h : 4 * h + 4].reshape(256, HALF))
        for j in range(28):
            for i in range(2):
                row = i * 28 + j
                update[i, :, j * BS + h * HALF : j * BS + (h + 1) * HALF] = tiles[
                    row * 8 : row * 8 + 4, :
                ]

    for k in pend:
        k.wait_send()


def move(a, b, c, to_a, to_b, to_c):
    to_a[...] = a[...]
    to_b[...] = b[...]
    to_c[...] = c[...]


def local(
    hidden_states,
    latent_grad,
    left_factor,
    right_factor,
    left_root,
    right_root,
    block_owner,
    block_slot,
):
    dtype_of = lambda key: BF16 if key[1] == 0 or PARTS[key[0]][1] == "m" else F32
    wide = sum(nj for first, nj in PAIRS if first == "x") * HALF
    bufs = [pltpu.VMEM(CHAIN[key], dtype_of(key)) for key in KEYS]
    scratch = bufs + bufs
    for width_of in (lambda w: ((2 * TOK, w), BF16), lambda w: ((LAT, w), F32)):
        scratch = scratch + [pltpu.VMEM(*width_of(part[3] * HALF)) for part in PARTS]
    scratch = scratch + [
        pltpu.VMEM((128 if part[1] == "x" else 64, part[3] * HALF), F32) for part in PARTS
    ]
    scratch = scratch + [
        pltpu.VMEM((2, TOK, LAT), BF16),
        pltpu.VMEM((2, LAT, 2 * TOK), BF16),
        pltpu.VMEM((2, 8, 32, HALF), F32),
        pltpu.VMEM((2, 7, 32, HALF), F32),
        pltpu.VMEM((8, 32, HALF), BF16),
        pltpu.VMEM((8, 32, HALF), BF16),
        pltpu.VMEM((8, 32, HALF), BF16),
        pltpu.VMEM((8, 32, HALF), BF16),
        pltpu.VMEM((4, 32, HALF), BF16),
        pltpu.VMEM((8, 4, 32, HALF), BF16),
        pltpu.VMEM((2, BS, BS), F32),
        pltpu.VMEM((8, 16, HALF), F32),
        pltpu.VMEM((8, 16, HALF), BF16),
        pltpu.VMEM((8, 16, HALF), BF16),
        pltpu.VMEM((8, 16, HALF), BF16),
        pltpu.VMEM((8, 16, HALF), BF16),
        pltpu.VMEM((8, 64, HALF), BF16),
        pltpu.VMEM((2, 32, BS), F32),
        pltpu.VMEM((2, 32, BS), F32),
        pltpu.VMEM((2, BS, BS), BF16),
        pltpu.VMEM((2, BS, BS), BF16),
        pltpu.VMEM((2, 128, wide), BF16),
        pltpu.VMEM((2, 7, 16, wide), BF16),
        pltpu.SemaphoreType.DMA((3, len(PARTS) + 1)),
        pltpu.SemaphoreType.DMA((len(KEYS),)),
        pltpu.SemaphoreType.DMA((len(KEYS),)),
        pltpu.SemaphoreType.DMA((2, 2, 7)),
        pltpu.SemaphoreType.DMA((6, 2, 7)),
        pltpu.SemaphoreType.DMA((4,)),
        pltpu.SemaphoreType.DMA((2, 2, 7)),
    ]
    vmem = pl.BlockSpec(memory_space=pltpu.VMEM)
    anywhere = pl.BlockSpec(memory_space=pl.ANY)
    results = pl.pallas_call(
        kernel,
        out_shape=(
            jax.ShapeDtypeStruct((2, 32, BS), F32),
            jax.ShapeDtypeStruct((2, 32, BS), F32),
            jax.ShapeDtypeStruct((2, 4, D), F32),
        ),
        in_specs=[anywhere] * 6 + [vmem, vmem],
        out_specs=(vmem, vmem, vmem),
        scratch_shapes=scratch,
        compiler_params=pltpu.CompilerParams(
            collective_id=0, has_side_effects=True, vmem_limit_bytes=56 * 1024 * 1024
        ),
    )(
        hidden_states,
        latent_grad,
        left_factor,
        right_factor,
        left_root,
        right_root,
        block_owner.reshape(1, 56),
        block_slot.reshape(1, 56),
    )
    return pl.pallas_call(
        move,
        out_shape=tuple(jax.ShapeDtypeStruct(r.shape, r.dtype) for r in results),
        in_specs=[vmem] * 3,
        out_specs=(vmem,) * 3,
    )(*results)


def solution(mesh):
    placed = (
        P(("replica", "shard"), None),
        P(("replica", "shard"), None),
        P("shard", "replica", None),
        P("shard", "replica", None),
        P("shard", None, None),
        P("shard", None, None),
        P(),
        P(),
    )
    return jax.shard_map(
        local,
        mesh=mesh,
        in_specs=placed,
        out_specs=(
            P("shard", "replica", None),
            P("shard", "replica", None),
            P(None, "shard", None),
        ),
        check_vma=False,
    )
```
